32 devices in a mesh: events: 2 (over x), shells: 16 (over z, y, core).
Axes of the slice: x: 2, y: 2, z: 4, core: 2. Of those that a mesh axis runs over, the one named last changes fastest.
Arguments:
- model: bfloat16 [1048576], P('shells'), may hold values from -6 to 6
- sensitivity: bfloat16 [16384, 64, 128], P(('events', 'shells')), may hold values from -0.1875 to 0.1875
- pick_block: int32 [16384], P(('events', 'shells')), may hold values from 0 to 1023, as said below
- cell_block: int32 [16384], P(('events', 'shells')), may hold values from 0 to 511
- blk_count: int32 [32], P(('events', 'shells')), may hold values from 128 to 512, as said below
- observed: float32 [131072], P(('events', 'shells')), may hold values from -6 to 6
- pick_weight: float32 [131072], P(('events', 'shells')), may hold values from 0.2 to 15
- station: int32 [131072], P(('events', 'shells')), may hold values from 0 to 2047
Outputs:
- gradient: float32 [1048576], P('shells')
- correction: float32 [2048], replicated
- weighted: float32 [131072], P(('events', 'shells'))
The draws below stay inside these ranges and needn't reach their ends.
Inputs may be any that keep to these rules, and one draw needn't show every extreme that they name: `blk_count`: each device uses its first slots; some device uses all 512 in every draw. The owner of a slot is pick_block // 64. Among the used slots of one device, at most 64 have one owner; in every event group some owner gets exactly 64 from every device of the group.
All inputs are finite; a program needn't handle non-finite values.
Results may differ from the reference program's by a relative error of at most 0.0026.
Values may be sent and summed in bfloat16 or wider, within the bound.
A program may use at most 64 MiB of HBM per device.

```python
import jax
import jax.numpy as jnp
from jax import lax

PICK_BLK = 64
CELL_BLK = 128
STATIONS = 2048
PBLK_DEV = 64
CBLK_DEV = 512
NBLK = 512
DEVS_ALL = 32
GROUP_PBLK = 1024
PICKS = 131072
CELLS = 1048576
SLOTS = 16384
PICK_CAP = 64
N_EVENTS = 2
N_SHELLS = 16


def station_table(key):
    return jax.random.randint(jax.random.fold_in(key, 7), (PICKS,), 0, STATIONS, dtype=jnp.int32)


def draw_station(key, part):
    return station_table(key)


def draw_observed(key, part):
    stations_of = station_table(key)
    offsets = jax.random.uniform(jax.random.fold_in(key, 8), (STATIONS,), jnp.float32, -2.0, 2.0)
    scatter_part = jnp.clip(jax.random.normal(jax.random.fold_in(key, 9), (PICKS,), jnp.float32), -4.0, 4.0)
    return offsets[stations_of] + 0.5 * scatter_part


def draw_pick_weight(key, part):
    rising = 1.0 + 2.0 * jnp.arange(PICKS, dtype=jnp.float32) / PICKS
    spread_part = jnp.exp(jax.random.uniform(jax.random.fold_in(key, 10), (PICKS,), jnp.float32, jnp.log(0.2), jnp.log(5.0)))
    return spread_part * rising


def draw_blk_count(key, part):
    counts = jax.random.randint(jax.random.fold_in(key, 11), (DEVS_ALL,), NBLK // 4, NBLK + 1, dtype=jnp.int32)
    shuffle = jax.random.permutation(jax.random.fold_in(key, 12), DEVS_ALL)
    return counts.at[shuffle[0]].set(NBLK)


def draw_pick_block(key, part):
    group_owner = jax.random.randint(jax.random.fold_in(key, 21), (N_EVENTS,), 0, N_SHELLS, dtype=jnp.int32)
    device_keys = jax.random.split(jax.random.fold_in(key, 22), DEVS_ALL)

    def one_device(dev_key, device):
        chosen = group_owner[device // N_SHELLS]
        order = jax.random.permutation(dev_key, (N_SHELLS - 1) * PICK_CAP)[:NBLK - PICK_CAP].astype(jnp.int32)
        others = order // PICK_CAP
        others = others + (others >= chosen).astype(jnp.int32)
        owners = jnp.concatenate([jnp.full((PICK_CAP,), chosen, dtype=jnp.int32), others])
        inside = jax.random.randint(jax.random.fold_in(dev_key, 1), (NBLK,), 0, PBLK_DEV, dtype=jnp.int32)
        return owners * PBLK_DEV + inside
    table = jax.vmap(one_device)(device_keys, jnp.arange(DEVS_ALL, dtype=jnp.int32))
    return table.reshape(SLOTS)


def touch_ends(entries, stream_key, smallest, high):
    longest = entries.shape.index(max(entries.shape))
    spots = []
    for shift in (0, 1):
        where = [jax.random.randint(jax.random.fold_in(stream_key, axis), (), 0, length) for axis, length in enumerate(entries.shape)]
        where[longest] = (where[longest] + shift) % entries.shape[longest]
        spots.append(tuple(where))
    return entries.at[spots[0]].set(smallest).at[spots[1]].set(high)


def steps_of(rng, dims, pieces, smallest, largest):
    factor_of, own = 1.0, jax.random.fold_in(rng, 6)
    for axis_at, blocks in pieces:
        steps = jnp.exp(jax.random.uniform(jax.random.fold_in(own, axis_at), (blocks,), jnp.float32, smallest / len(pieces), largest / len(pieces)))
        factor_of = factor_of * jnp.repeat(steps, dims[axis_at] // blocks).reshape([-1 if axis == axis_at else 1 for axis in range(len(dims))])
    return factor_of


def scatter_about(stream_key, dims, width, reach, shards=(), kind=jnp.bfloat16):
    values = width * jax.random.normal(stream_key, dims, jnp.float32)
    if shards:
        values = values * steps_of(stream_key, dims, shards, -0.22, 0.18)
    return jnp.clip(values, -reach, reach).astype(kind)


def setup_inputs(seed: int = 0) -> dict:
    key_of = jax.random.split(jax.random.key(seed), 9)
    return {
        "model": scatter_about(key_of[0], (CELLS,), 1.0, 6.0, ((0, 16),)),
        "sensitivity": scatter_about(key_of[1], (SLOTS, PICK_BLK, CELL_BLK), (CELL_BLK * max(1, NBLK // PBLK_DEV)) ** -0.5, 0.1875, ((0, 32),)),
        "pick_block": draw_pick_block(jax.random.fold_in(key_of[8], 71), 0),
        "cell_block": touch_ends(jax.random.randint(key_of[3], (SLOTS,), 0, CBLK_DEV), jax.random.fold_in(key_of[3], 1), 0, CBLK_DEV - 1).astype(jnp.int32),
        "blk_count": draw_blk_count(jax.random.fold_in(key_of[8], 71), 0),
        "observed": draw_observed(jax.random.fold_in(key_of[8], 71), 0),
        "pick_weight": draw_pick_weight(jax.random.fold_in(key_of[8], 71), 0),
        "station": draw_station(jax.random.fold_in(key_of[8], 71), 0),
    }


def reference(model, sensitivity, pick_block, cell_block, blk_count, observed, pick_weight, station):
    n_devices = N_EVENTS * N_SHELLS
    blocks_all = sensitivity.reshape(n_devices, NBLK, PICK_BLK, CELL_BLK)
    pick_rows = pick_block.reshape(n_devices, NBLK)
    cell_rows = cell_block.reshape(n_devices, NBLK)
    model_shells = model.reshape(N_SHELLS, CBLK_DEV, CELL_BLK)
    device_ids = jnp.arange(n_devices, dtype=jnp.int32)
    shell_ids = device_ids % N_SHELLS
    event_ids = device_ids // N_SHELLS
    living = (jnp.arange(NBLK, dtype=jnp.int32)[None, :] < blk_count[:, None]).astype(jnp.float32)

    def forward(packed):
        blocks, picks_of, cells_of, shell_id, alive = packed
        rows_used = jnp.take(model_shells, shell_id, axis=0)[cells_of].astype(jnp.float32)
        values = jnp.einsum("kpc,kc->kp", blocks.astype(jnp.float32), rows_used) * alive[:, None]
        return jax.ops.segment_sum(values, picks_of, num_segments=GROUP_PBLK)

    partials = lax.map(forward, (blocks_all, pick_rows, cell_rows, shell_ids, living))
    predicted = partials.reshape(N_EVENTS, N_SHELLS, GROUP_PBLK * PICK_BLK).sum(axis=1).reshape(PICKS)
    misfit = observed - predicted
    numer = jax.ops.segment_sum(pick_weight * misfit, station, num_segments=STATIONS)
    denom = jax.ops.segment_sum(pick_weight, station, num_segments=STATIONS)
    correction = numer / (denom + 1.0)
    weighted = pick_weight * (misfit - correction[station])
    weighted_half = weighted.astype(jnp.bfloat16)
    residual_groups = weighted_half.reshape(N_EVENTS, GROUP_PBLK, PICK_BLK)

    def backward(packed):
        blocks, picks_of, cells_of, event_id, alive = packed
        resid_rows = jnp.take(residual_groups, event_id, axis=0)[picks_of].astype(jnp.float32)
        terms = jnp.einsum("kpc,kp->kc", blocks.astype(jnp.float32), resid_rows) * alive[:, None]
        return jax.ops.segment_sum(terms, cells_of, num_segments=CBLK_DEV)

    grads = lax.map(backward, (blocks_all, pick_rows, cell_rows, event_ids, living))
    gradient = grads.reshape(N_EVENTS, N_SHELLS, CBLK_DEV * CELL_BLK).sum(axis=0).reshape(CELLS)
    return gradient, correction, weighted
```

```python
import functools

import jax
import jax.numpy as jnp
from jax import lax
from jax.experimental import pallas as pl
from jax.experimental.pallas import tpu as pltpu
from jax.sharding import PartitionSpec as P

PICK_BLK = 64
CELL_BLK = 128
STATIONS = 2048
LANES = 128
GROUP = 16
STEPS = 8
MESH = pl.DeviceIdType.MESH
F32 = jnp.float32
BF16 = jnp.bfloat16


def dot_nn(a, b):
    return lax.dot_general(a, b, (((1,), (0,)), ((), ())), preferred_element_type=F32)


def dot_nt(a, b):
    return lax.dot_general(a, b, (((1,), (1,)), ((), ())), preferred_element_type=F32)


def dot_tn(a, b):
    return lax.dot_general(a, b, (((0,), (0,)), ((), ())), preferred_element_type=F32)


def parts_of(x, count):
    parts = []
    for _ in range(count):
        part = x.astype(BF16)
        parts.append(part)
        x = x - part.astype(F32)
    return parts


def one_hot(rows, index_row, keep=None):
    shape = (rows, index_row.shape[1])
    hit = lax.broadcasted_iota(jnp.int32, shape, 0) == index_row
    if keep is not None:
        hit = jnp.logical_and(hit, keep)
    return jnp.where(hit, 1.0, 0.0).astype(BF16)


def diagonal_mask(j):
    row = lax.broadcasted_iota(jnp.int32, (GROUP, LANES), 0)
    lane = lax.broadcasted_iota(jnp.int32, (GROUP, LANES), 1)
    return row == 2 * j + lane // PICK_BLK


def swap_halves(x):
    return pltpu.roll(x, PICK_BLK, 1)


def halves(rows):
    return lax.broadcasted_iota(jnp.int32, (rows, LANES), 1) < PICK_BLK


def forward_kernel(count_ref, blocks_ref, model_ref, pick_ref, cell_ref, out_ref, gathered, values):
    step = pl.program_id(0)
    slots = values.shape[0]
    per_step = slots // STEPS

    @pl.when(step == 0)
    def _():
        hot = one_hot(model_ref.shape[0], cell_ref[...])
        gathered[...] = dot_tn(hot, model_ref[...]).astype(BF16)

    for g in range(per_step // GROUP):
        first = pl.multiple_of(step * per_step + g * GROUP, GROUP)
        rows = gathered[pl.ds(first, GROUP), :]
        block = blocks_ref[g * GROUP * PICK_BLK:(g + 1) * GROUP * PICK_BLK, :]
        full = dot_nt(rows, block)
        total = jnp.zeros((GROUP, LANES), F32)
        for j in range(GROUP // 2):
            total = total + jnp.where(diagonal_mask(j), full[:, j * LANES:(j + 1) * LANES], 0.0)
        values[pl.ds(first, GROUP), :] = total

    @pl.when(step == STEPS - 1)
    def _():
        v = values[...]
        v = v + swap_halves(v)
        terms = jnp.concatenate(parts_of(v, 2), axis=1)
        pick = pick_ref[...]
        alive = lax.broadcasted_iota(jnp.int32, (1, slots), 1) < count_ref[0]
        rows = out_ref.shape[0]
        low = dot_nn(one_hot(rows, pick // 2, jnp.logical_and(alive, pick % 2 == 0)), terms)
        high = dot_nn(one_hot(rows, pick // 2, jnp.logical_and(alive, pick % 2 == 1)), terms)
        both = jnp.where(
            lax.broadcasted_iota(jnp.int32, (rows, 2 * LANES), 1) % LANES < PICK_BLK, low, high
        )
        out_ref[...] = both[:, :LANES] + both[:, LANES:]


def backward_kernel(count_ref, blocks_ref, resid_ref, pick_ref, cell_ref, out_ref, gathered, terms):
    step = pl.program_id(0)
    slots = terms.shape[0]
    per_step = slots // STEPS

    @pl.when(step == 0)
    def _():
        pick = pick_ref[...]
        rows = resid_ref.shape[0]
        low = dot_tn(one_hot(rows, pick // 2, pick % 2 == 0), resid_ref[...])
        high = dot_tn(one_hot(rows, pick // 2, pick % 2 == 1), resid_ref[...])
        picked = jnp.where(halves(slots), low, high)
        gathered[...] = picked + swap_halves(picked)

    for g in range(per_step // GROUP):
        first = pl.multiple_of(step * per_step + g * GROUP, GROUP)
        rows = gathered[pl.ds(first, GROUP), :]
        spread = jnp.concatenate(
            [jnp.where(diagonal_mask(j), rows, 0.0).astype(BF16) for j in range(GROUP // 2)], axis=1
        )
        block = blocks_ref[g * GROUP * PICK_BLK:(g + 1) * GROUP * PICK_BLK, :]
        terms[pl.ds(first, GROUP), :] = dot_nn(spread, block)

    @pl.when(step == STEPS - 1)
    def _():
        alive = lax.broadcasted_iota(jnp.int32, (1, slots), 1) < count_ref[0]
        hot = one_hot(out_ref.shape[0], cell_ref[...], alive)
        both = dot_nn(hot, jnp.concatenate(parts_of(terms[...], 2), axis=1))
        out_ref[...] = both[:, :LANES] + both[:, LANES:]


def middle_kernel(
    n_events, n_shells,
    partial_ref, observed_ref, weight_ref, station_ref,
    resid_ref, correction_ref, weighted_ref,
    landed, low_hot, spread, sums_out, sums_in, fitted,
    send_a, recv_a, send_b, recv_b, send_c, recv_c, send_d, recv_d,
):
    event = lax.axis_index("events")
    shell = lax.axis_index("shells")
    n_devices = n_events * n_shells
    mine = event * n_shells + shell
    rows = observed_ref.shape[0]
    n_high = sums_out.shape[0]

    barrier = pltpu.get_barrier_semaphore()

    def greet(i, carry):
        other = lax.rem(mine + i, n_devices)
        pl.semaphore_signal(
            barrier, inc=1, device_id=(other // n_shells, lax.rem(other, n_shells)),
            device_id_type=MESH,
        )
        return carry

    lax.fori_loop(1, n_devices, greet, 0)
    pl.semaphore_wait(barrier, n_devices - 1)

    def shell_at(i):
        return lax.rem(shell + i, n_shells)

    def shell_from(i):
        return lax.rem(shell + n_shells - i, n_shells)

    def partial_copy(i, source):
        other = shell_at(i)
        return pltpu.make_async_remote_copy(
            src_ref=partial_ref.at[pl.ds(pl.multiple_of(other * rows, rows), rows), :],
            dst_ref=landed.at[source],
            send_sem=send_a.at[i],
            recv_sem=recv_a.at[source],
            device_id=(event, other),
            device_id_type=MESH,
        )

    def start_partial(i, carry):
        partial_copy(i, shell).start()
        return carry

    lax.fori_loop(1, n_shells, start_partial, 0)

    station = station_ref[...]
    high, low = station // LANES, lax.rem(station, LANES)
    for r in range(rows):
        low_hot[:, r * LANES:(r + 1) * LANES] = one_hot(LANES, low[r:r + 1, :])
    high_id = lax.broadcasted_iota(jnp.int32, (n_high, LANES), 0)

    def station_sums(x):
        pieces = parts_of(x, 3)
        for r in range(rows):
            hit = high_id == high[r:r + 1, :]
            for k in range(3):
                piece = pieces[k][r:r + 1, :].astype(F32)
                spread[k * n_high:(k + 1) * n_high, r * LANES:(r + 1) * LANES] = jnp.where(
                    hit, piece, 0.0
                ).astype(BF16)
        out = dot_nt(spread[...], low_hot[...])
        return out[:n_high] + (out[n_high:2 * n_high] + out[2 * n_high:])

    weight = weight_ref[...]
    denom = station_sums(weight)
    for h in range(n_high):
        sums_out[h, 1:2, :] = denom[h:h + 1, :]

    def take_partial(i, total):
        source = shell_from(i)
        partial_copy(i, source).wait_recv()
        return total + landed[source]

    own = partial_ref[pl.ds(pl.multiple_of(shell * rows, rows), rows), :]
    predicted = lax.fori_loop(1, n_shells, take_partial, own)
    misfit = observed_ref[...] - predicted
    numer = station_sums(weight * misfit)
    for h in range(n_high):
        sums_out[h, 0:1, :] = numer[h:h + 1, :]

    def sums_copy(i, source):
        other = lax.rem(mine + i, n_devices)
        other_shell = lax.rem(other, n_shells)
        return pltpu.make_async_remote_copy(
            src_ref=sums_out.at[other_shell],
            dst_ref=sums_in.at[source],
            send_sem=send_b.at[i],
            recv_sem=recv_b.at[source],
            device_id=(other // n_shells, other_shell),
            device_id_type=MESH,
        )

    def start_sums(i, carry):
        sums_copy(i, mine).start()
        return carry

    lax.fori_loop(1, n_devices, start_sums, 0)
    sums_in[mine] = sums_out[shell]

    def wait_sums(i, carry):
        sums_copy(i, lax.rem(mine + n_devices - i, n_devices)).wait_recv()
        return carry

    lax.fori_loop(1, n_devices, wait_sums, 0)

    def add_sums(d, total):
        return total + sums_in[d]

    total = lax.fori_loop(1, n_devices, add_sums, sums_in[0])
    fitted[shell] = total[0:1, :] / (total[1:2, :] + 1.0)

    def fitted_copy(i, source):
        return pltpu.make_async_remote_copy(
            src_ref=fitted.at[source],
            dst_ref=fitted.at[source],
            send_sem=send_c.at[i],
            recv_sem=recv_c.at[source],
            device_id=(event, shell_at(i)),
            device_id_type=MESH,
        )

    def start_fitted(i, carry):
        fitted_copy(i, shell).start()
        return carry

    def wait_fitted(i, carry):
        fitted_copy(i, shell_from(i)).wait_recv()
        return carry

    lax.fori_loop(1, n_shells, start_fitted, 0)
    lax.fori_loop(1, n_shells, wait_fitted, 0)

    correction = jnp.concatenate([fitted[h] for h in range(n_high)], axis=0)
    correction_ref[...] = correction[:correction_ref.shape[0]]
    pieces = jnp.concatenate(parts_of(correction, 3), axis=0)
    wide = dot_nn(pieces, low_hot[...])
    wide = wide[:n_high] + (wide[n_high:2 * n_high] + wide[2 * n_high:])
    picked = []
    for r in range(rows):
        hit = high_id == high[r:r + 1, :]
        picked.append(
            jnp.sum(jnp.where(hit, wide[:, r * LANES:(r + 1) * LANES], 0.0), axis=0, keepdims=True)
        )
    weighted = weight * (misfit - jnp.concatenate(picked, axis=0))
    weighted_ref[...] = weighted
    resid_ref[shell] = weighted.astype(BF16)

    def resid_copy(i, source):
        return pltpu.make_async_remote_copy(
            src_ref=resid_ref.at[source],
            dst_ref=resid_ref.at[source],
            send_sem=send_d.at[i],
            recv_sem=recv_d.at[source],
            device_id=(event, shell_at(i)),
            device_id_type=MESH,
        )

    def start_resid(i, carry):
        resid_copy(i, shell).start()
        return carry

    def wait_resid(i, carry):
        resid_copy(i, shell_from(i)).wait_recv()
        return carry

    lax.fori_loop(1, n_shells, start_resid, 0)
    lax.fori_loop(1, n_shells, wait_resid, 0)

    def sent(i, carry):
        partial_copy(i, shell).wait_send()
        fitted_copy(i, shell).wait_send()
        resid_copy(i, shell).wait_send()
        return carry

    def sums_sent(i, carry):
        sums_copy(i, mine).wait_send()
        return carry

    lax.fori_loop(1, n_shells, sent, 0)
    lax.fori_loop(1, n_devices, sums_sent, 0)


def local(n_events, n_shells, model, sensitivity, pick_block, cell_block, blk_count, observed, pick_weight, station):
    slots = sensitivity.shape[0]
    cells = model.shape[0] // CELL_BLK
    rows = observed.shape[0] // LANES
    group_rows = rows * n_shells
    high_rows = STATIONS // LANES
    n_high = max(high_rows, n_shells)
    blocks = sensitivity.reshape(slots * PICK_BLK, CELL_BLK)
    pick = pick_block.reshape(1, slots)
    cell = cell_block.reshape(1, slots)
    chunk = slots // STEPS * PICK_BLK
    whole = lambda *shape: pl.BlockSpec(shape, lambda i: (0,) * len(shape))
    params = pltpu.CompilerParams(
        dimension_semantics=("arbitrary",), vmem_limit_bytes=48 * 1024 * 1024
    )
    cost = pl.CostEstimate(
        flops=2 * slots * PICK_BLK * CELL_BLK,
        bytes_accessed=2 * slots * PICK_BLK * CELL_BLK,
        transcendentals=0,
    )
    count_spec = pl.BlockSpec(memory_space=pltpu.SMEM)
    blocks_spec = pl.BlockSpec((chunk, CELL_BLK), lambda i: (i, 0))

    partial = pl.pallas_call(
        forward_kernel,
        grid=(STEPS,),
        out_shape=jax.ShapeDtypeStruct((group_rows, LANES), F32),
        in_specs=[
            count_spec, blocks_spec, whole(cells, CELL_BLK), whole(1, slots), whole(1, slots),
        ],
        out_specs=whole(group_rows, LANES),
        scratch_shapes=[pltpu.VMEM((slots, CELL_BLK), BF16), pltpu.VMEM((slots, LANES), F32)],
        compiler_params=params,
        cost_estimate=cost,
    )(blk_count, blocks, model.reshape(cells, CELL_BLK), pick, cell)

    n_devices = n_events * n_shells
    dma = lambda n: pltpu.SemaphoreType.DMA((n,))
    resid, correction, weighted = pl.pallas_call(
        functools.partial(middle_kernel, n_events, n_shells),
        out_shape=(
            jax.ShapeDtypeStruct((n_shells, rows, LANES), BF16),
            jax.ShapeDtypeStruct((high_rows, LANES), F32),
            jax.ShapeDtypeStruct((rows, LANES), F32),
        ),
        in_specs=[pl.BlockSpec(memory_space=pltpu.VMEM)] * 4,
        out_specs=(pl.BlockSpec(memory_space=pltpu.VMEM),) * 3,
        scratch_shapes=[
            pltpu.VMEM((n_shells, rows, LANES), F32),
            pltpu.VMEM((LANES, rows * LANES), BF16),
            pltpu.VMEM((3 * n_high, rows * LANES), BF16),
            pltpu.VMEM((n_high, 2, LANES), F32),
            pltpu.VMEM((n_devices, 2, LANES), F32),
            pltpu.VMEM((n_high, 1, LANES), F32),
            dma(n_shells), dma(n_shells), dma(n_devices), dma(n_devices),
            dma(n_shells), dma(n_shells), dma(n_shells), dma(n_shells),
        ],
        compiler_params=pltpu.CompilerParams(
            collective_id=0, has_side_effects=True, vmem_limit_bytes=48 * 1024 * 1024
        ),
    )(
        partial,
        observed.reshape(rows, LANES),
        pick_weight.reshape(rows, LANES),
        station.reshape(rows, LANES),
    )

    grads = pl.pallas_call(
        backward_kernel,
        grid=(STEPS,),
        out_shape=jax.ShapeDtypeStruct((cells, CELL_BLK), F32),
        in_specs=[
            count_spec, blocks_spec, whole(group_rows, LANES), whole(1, slots), whole(1, slots),
        ],
        out_specs=whole(cells, CELL_BLK),
        scratch_shapes=[pltpu.VMEM((slots, LANES), F32), pltpu.VMEM((slots, CELL_BLK), F32)],
        compiler_params=params,
        cost_estimate=cost,
    )(blk_count, blocks, resid.reshape(group_rows, LANES), pick, cell)

    if n_events == 2:
        other = lax.ppermute(grads, "events", [(0, 1), (1, 0)])
        gradient = grads + other
    else:
        gradient = lax.psum(grads, "events")
    return (gradient.reshape(-1), correction.reshape(-1), weighted.reshape(-1))


def solution(mesh):
    every = P(("events", "shells"))
    placed = (P("shells"), P(("events", "shells"), None, None)) + (every,) * 6
    return jax.shard_map(
        functools.partial(local, mesh.shape["events"], mesh.shape["shells"]),
        mesh=mesh,
        in_specs=placed,
        out_specs=(P("shells"), P(), every),
        check_vma=False,
    )
```

```python
import functools

import jax
import jax.numpy as jnp
from jax import lax
from jax.experimental import pallas as pl
from jax.experimental.pallas import tpu as pltpu
from jax.sharding import PartitionSpec as P

PICK_BLK = 64
CELL_BLK = 128
STATIONS = 2048
LANES = 128
GROUP = 16
CHUNKS = 4
MESH = pl.DeviceIdType.MESH
F32 = jnp.float32
BF16 = jnp.bfloat16


def dot_nn(a, b):
    return lax.dot_general(a, b, (((1,), (0,)), ((), ())), preferred_element_type=F32)


def dot_nt(a, b):
    return lax.dot_general(a, b, (((1,), (1,)), ((), ())), preferred_element_type=F32)


def parts_of(x, count):
    parts = []
    for _ in range(count):
        part = x.astype(BF16)
        parts.append(part)
        x = x - part.astype(F32)
    return parts


def one_hot(rows, index_row):
    shape = (rows, index_row.shape[1])
    hit = lax.broadcasted_iota(jnp.int32, shape, 0) == index_row
    return jnp.where(hit, 1.0, 0.0).astype(BF16)


def diagonal_mask(j):
    row = lax.broadcasted_iota(jnp.int32, (GROUP, LANES), 0)
    lane = lax.broadcasted_iota(jnp.int32, (GROUP, LANES), 1)
    return row == 2 * j + lane // PICK_BLK


def swap_halves(x):
    return pltpu.roll(x, PICK_BLK, 1)


def whole_kernel(
    n_events, n_shells,
    count_ref, blocks_ref, model_ref, pick_ref, cell_ref, observed_ref, weight_ref, station_ref,
    gradient_ref, correction_ref, weighted_ref,
    blocks, pick_hot, pick_hot_t, cell_hot, model_rows, slot_rows, values, partial, landed,
    low_hot, spread, sums_out, sums_in, fitted, resid, grads_out, grads_in,
    load_sem, send_a, recv_a, send_b, recv_b, send_c, recv_c, send_d, recv_d, send_e, recv_e,
):
    event = lax.axis_index("events")
    shell = lax.axis_index("shells")
    n_devices = n_events * n_shells
    mine = event * n_shells + shell
    rows = observed_ref.shape[0]
    n_high = sums_out.shape[0]
    slots = values.shape[0]
    cells = model_ref.shape[0]
    group_rows = partial.shape[0]
    per_chunk = slots // CHUNKS
    chunk_rows = per_chunk * PICK_BLK

    def after(x, i, n):
        return jnp.where(x + i >= n, x + i - n, x + i)

    def before(x, i, n):
        return jnp.where(x >= i, x - i, x + n - i)

    def load(c):
        part = pl.ds(pl.multiple_of(c * chunk_rows, chunk_rows), chunk_rows)
        return pltpu.make_async_copy(blocks_ref.at[part, :], blocks.at[part, :], load_sem.at[c])

    for c in range(CHUNKS):
        load(c).start()

    barrier = pltpu.get_barrier_semaphore()

    def greet_shell(i, carry):
        for j in range(n_events):
            pl.semaphore_signal(
                barrier, inc=1,
                device_id=(after(event, j, n_events), after(shell, i, n_shells)),
                device_id_type=MESH,
            )
        return carry

    for j in range(1, n_events):
        pl.semaphore_signal(
            barrier, inc=1, device_id=(after(event, j, n_events), shell), device_id_type=MESH
        )
    lax.fori_loop(1, n_shells, greet_shell, 0)

    alive = lax.broadcasted_iota(jnp.int32, (1, slots), 1) < count_ref[0]
    pick = jnp.where(alive, pick_ref[...], -2)
    cell = jnp.where(alive, cell_ref[...], -2)
    cell_column = jnp.transpose(jnp.broadcast_to(cell, (LANES, slots)))
    lane = lax.broadcasted_iota(jnp.int32, (slots, LANES), 1)
    found = jnp.zeros((slots, CELL_BLK), F32)
    for b in range(cells // LANES):
        hot = jnp.where(lane + b * LANES == cell_column, 1.0, 0.0).astype(BF16)
        found = found + dot_nn(hot, model_ref[b * LANES:(b + 1) * LANES, :])
    model_rows[...] = found.astype(BF16)
    pick_row = lax.shift_right_arithmetic(pick, 1)
    pick_hot[...] = one_hot(group_rows, pick_row)
    cell_hot[...] = one_hot(cells, cell)
    pick_column = jnp.transpose(jnp.broadcast_to(pick, (LANES, slots)))
    half = (pick_column & 1) == lane // PICK_BLK
    pick_column = lax.shift_right_arithmetic(pick_column, 1)
    for b in range(group_rows // LANES):
        pick_hot_t[:, b * LANES:(b + 1) * LANES] = jnp.where(
            lane + b * LANES == pick_column, 1.0, 0.0
        ).astype(BF16)

    def forward_chunk(c, carry):
        load(c).wait()
        for g in range(per_chunk // GROUP):
            first = pl.multiple_of(c * per_chunk + g * GROUP, GROUP)
            block = blocks[pl.ds(pl.multiple_of(first * PICK_BLK, GROUP * PICK_BLK), GROUP * PICK_BLK), :]
            full = dot_nt(model_rows[pl.ds(first, GROUP), :], block)
            total = jnp.zeros((GROUP, LANES), F32)
            for j in range(GROUP // 2):
                total = total + jnp.where(diagonal_mask(j), full[:, j * LANES:(j + 1) * LANES], 0.0)
            values[pl.ds(first, GROUP), :] = total
        return carry

    lax.fori_loop(0, CHUNKS, forward_chunk, 0)
    v = values[...]
    v = jnp.where(half, v + swap_halves(v), 0.0)
    both = dot_nn(pick_hot[...], jnp.concatenate(parts_of(v, 2), axis=1))
    partial[...] = both[:, :LANES] + both[:, LANES:]

    pl.semaphore_wait(barrier, n_devices - 1)

    def partial_copy(i, source):
        other = after(shell, i, n_shells)
        return pltpu.make_async_remote_copy(
            src_ref=partial.at[pl.ds(pl.multiple_of(other * rows, rows), rows), :],
            dst_ref=landed.at[source],
            send_sem=send_a.at[i],
            recv_sem=recv_a.at[source],
            device_id=(event, other),
            device_id_type=MESH,
        )

    def start_partial(i, carry):
        partial_copy(i, shell).start()
        return carry

    lax.fori_loop(1, n_shells, start_partial, 0)

    station = station_ref[...]
    high, low = station // LANES, lax.rem(station, LANES)
    for r in range(rows):
        low_hot[:, r * LANES:(r + 1) * LANES] = one_hot(LANES, low[r:r + 1, :])
    high_id = lax.broadcasted_iota(jnp.int32, (n_high, LANES), 0)

    def station_sums(x):
        pieces = parts_of(x, 3)
        for r in range(rows):
            hit = high_id == high[r:r + 1, :]
            for k in range(3):
                piece = pieces[k][r:r + 1, :].astype(F32)
                spread[k * n_high:(k + 1) * n_high, r * LANES:(r + 1) * LANES] = jnp.where(
                    hit, piece, 0.0
                ).astype(BF16)
        out = dot_nt(spread[...], low_hot[...])
        return out[:n_high] + (out[n_high:2 * n_high] + out[2 * n_high:])

    weight = weight_ref[...]
    denom = station_sums(weight)
    for h in range(n_high):
        sums_out[h, 1:2, :] = denom[h:h + 1, :]

    def take_partial(i, total):
        source = before(shell, i, n_shells)
        partial_copy(i, source).wait_recv()
        return total + landed[source]

    own = partial[pl.ds(pl.multiple_of(shell * rows, rows), rows), :]
    predicted = lax.fori_loop(1, n_shells, take_partial, own)
    misfit = observed_ref[...] - predicted
    numer = station_sums(weight * misfit)
    for h in range(n_high):
        sums_out[h, 0:1, :] = numer[h:h + 1, :]

    def sums_copy(i, j, source):
        other = after(shell, i, n_shells)
        return pltpu.make_async_remote_copy(
            src_ref=sums_out.at[other],
            dst_ref=sums_in.at[source],
            send_sem=send_b.at[i * n_events + j],
            recv_sem=recv_b.at[source],
            device_id=(after(event, j, n_events), other),
            device_id_type=MESH,
        )

    def sums_from(i, j):
        return before(event, j, n_events) * n_shells + before(shell, i, n_shells)

    def start_sums(i, carry):
        for j in range(n_events):
            sums_copy(i, j, mine).start()
        return carry

    def wait_sums(i, carry):
        for j in range(n_events):
            sums_copy(i, j, sums_from(i, j)).wait_recv()
        return carry

    for j in range(1, n_events):
        sums_copy(0, j, mine).start()
    lax.fori_loop(1, n_shells, start_sums, 0)
    sums_in[mine] = sums_out[shell]
    for j in range(1, n_events):
        sums_copy(0, j, sums_from(0, j)).wait_recv()
    lax.fori_loop(1, n_shells, wait_sums, 0)

    total = jnp.sum(sums_in[...], axis=0)
    fitted[shell] = total[0:1, :] / (total[1:2, :] + 1.0)

    def fitted_copy(i, source):
        return pltpu.make_async_remote_copy(
            src_ref=fitted.at[source],
            dst_ref=fitted.at[source],
            send_sem=send_c.at[i],
            recv_sem=recv_c.at[source],
            device_id=(event, after(shell, i, n_shells)),
            device_id_type=MESH,
        )

    def start_fitted(i, carry):
        fitted_copy(i, shell).start()
        return carry

    def wait_fitted(i, carry):
        fitted_copy(i, before(shell, i, n_shells)).wait_recv()
        return carry

    lax.fori_loop(1, n_shells, start_fitted, 0)
    lax.fori_loop(1, n_shells, wait_fitted, 0)

    correction = jnp.concatenate([fitted[h] for h in range(n_high)], axis=0)
    correction_ref[...] = correction[:correction_ref.shape[0]]
    pieces = jnp.concatenate(parts_of(correction, 3), axis=0)
    wide = dot_nn(pieces, low_hot[...])
    wide = wide[:n_high] + (wide[n_high:2 * n_high] + wide[2 * n_high:])
    picked = []
    for r in range(rows):
        hit = high_id == high[r:r + 1, :]
        picked.append(
            jnp.sum(jnp.where(hit, wide[:, r * LANES:(r + 1) * LANES], 0.0), axis=0, keepdims=True)
        )
    weighted = weight * (misfit - jnp.concatenate(picked, axis=0))
    weighted_ref[...] = weighted
    resid[shell] = weighted.astype(BF16)

    def resid_copy(i, source):
        return pltpu.make_async_remote_copy(
            src_ref=resid.at[source],
            dst_ref=resid.at[source],
            send_sem=send_d.at[i],
            recv_sem=recv_d.at[source],
            device_id=(event, after(shell, i, n_shells)),
            device_id_type=MESH,
        )

    def start_resid(i, carry):
        resid_copy(i, shell).start()
        return carry

    def wait_resid(i, carry):
        resid_copy(i, before(shell, i, n_shells)).wait_recv()
        return carry

    lax.fori_loop(1, n_shells, start_resid, 0)
    lax.fori_loop(1, n_shells, wait_resid, 0)

    found = dot_nn(pick_hot_t[...], resid[...].reshape(group_rows, LANES))
    found = jnp.where(half, found, 0.0)
    slot_rows[...] = found + swap_halves(found)

    def backward_chunk(c, carry):
        for g in range(per_chunk // GROUP):
            first = pl.multiple_of(c * per_chunk + g * GROUP, GROUP)
            picked = slot_rows[pl.ds(first, GROUP), :]
            wide = jnp.concatenate(
                [jnp.where(diagonal_mask(j), picked, 0.0).astype(BF16) for j in range(GROUP // 2)],
                axis=1,
            )
            block = blocks[pl.ds(pl.multiple_of(first * PICK_BLK, GROUP * PICK_BLK), GROUP * PICK_BLK), :]
            values[pl.ds(first, GROUP), :] = dot_nn(wide, block)
        return carry

    lax.fori_loop(0, CHUNKS, backward_chunk, 0)
    terms = jnp.concatenate(parts_of(values[...], 2), axis=1)
    part = cells // CHUNKS

    def grads_copy(c):
        piece = pl.ds(c * part, part)
        return pltpu.make_async_remote_copy(
            src_ref=grads_out.at[piece, :],
            dst_ref=grads_in.at[piece, :],
            send_sem=send_e.at[c],
            recv_sem=recv_e.at[c],
            device_id=(1 - event, shell),
            device_id_type=MESH,
        )

    for c in range(CHUNKS):
        both = dot_nn(cell_hot[c * part:(c + 1) * part, :], terms)
        grads = both[:, :LANES] + both[:, LANES:]
        if n_events == 2:
            grads_out[c * part:(c + 1) * part, :] = grads.astype(BF16)
            grads_copy(c).start()
        else:
            gradient_ref[c * part:(c + 1) * part, :] = grads

    def sent(i, carry):
        partial_copy(i, shell).wait_send()
        fitted_copy(i, shell).wait_send()
        resid_copy(i, shell).wait_send()
        for j in range(n_events):
            sums_copy(i, j, mine).wait_send()
        return carry

    for j in range(1, n_events):
        sums_copy(0, j, mine).wait_send()
    lax.fori_loop(1, n_shells, sent, 0)
    if n_events == 2:
        for c in range(CHUNKS):
            grads_copy(c).wait_recv()
            piece = slice(c * part, (c + 1) * part)
            gradient_ref[piece, :] = grads_out[piece, :].astype(F32) + grads_in[piece, :].astype(F32)
        for c in range(CHUNKS):
            grads_copy(c).wait_send()


def local(n_events, n_shells, model, sensitivity, pick_block, cell_block, blk_count, observed, pick_weight, station):
    slots = sensitivity.shape[0]
    cells = model.shape[0] // CELL_BLK
    rows = observed.shape[0] // LANES
    group_rows = rows * n_shells
    high_rows = STATIONS // LANES
    n_high = max(high_rows, n_shells)
    n_devices = n_events * n_shells
    dma = lambda n: pltpu.SemaphoreType.DMA((n,))
    vmem = pl.BlockSpec(memory_space=pltpu.VMEM)
    gradient, correction, weighted = pl.pallas_call(
        functools.partial(whole_kernel, n_events, n_shells),
        out_shape=(
            jax.ShapeDtypeStruct((cells, CELL_BLK), F32),
            jax.ShapeDtypeStruct((high_rows, LANES), F32),
            jax.ShapeDtypeStruct((rows, LANES), F32),
        ),
        in_specs=[pl.BlockSpec(memory_space=pltpu.SMEM), pl.BlockSpec(memory_space=pl.ANY)]
        + [vmem] * 6,
        out_specs=(vmem,) * 3,
        scratch_shapes=[
            pltpu.VMEM((slots * PICK_BLK, CELL_BLK), BF16),
            pltpu.VMEM((group_rows, slots), BF16),
            pltpu.VMEM((slots, group_rows), BF16),
            pltpu.VMEM((cells, slots), BF16),
            pltpu.VMEM((slots, CELL_BLK), BF16),
            pltpu.VMEM((slots, LANES), F32),
            pltpu.VMEM((slots, LANES), F32),
            pltpu.VMEM((group_rows, LANES), F32),
            pltpu.VMEM((n_shells, rows, LANES), F32),
            pltpu.VMEM((LANES, rows * LANES), BF16),
            pltpu.VMEM((3 * n_high, rows * LANES), BF16),
            pltpu.VMEM((n_high, 2, LANES), F32),
            pltpu.VMEM((n_devices, 2, LANES), F32),
            pltpu.VMEM((n_high, 1, LANES), F32),
            pltpu.VMEM((n_shells, rows, LANES), BF16),
            pltpu.VMEM((cells, CELL_BLK), BF16),
            pltpu.VMEM((cells, CELL_BLK), BF16),
            dma(CHUNKS),
            dma(n_shells), dma(n_shells), dma(n_devices), dma(n_devices),
            dma(n_shells), dma(n_shells), dma(n_shells), dma(n_shells),
            dma(CHUNKS), dma(CHUNKS),
        ],
        compiler_params=pltpu.CompilerParams(
            collective_id=0, has_side_effects=True, vmem_limit_bytes=60 * 1024 * 1024
        ),
    )(
        blk_count,
        sensitivity.reshape(slots * PICK_BLK, CELL_BLK),
        model.reshape(cells, CELL_BLK),
        pick_block.reshape(1, slots),
        cell_block.reshape(1, slots),
        observed.reshape(rows, LANES),
        pick_weight.reshape(rows, LANES),
        station.reshape(rows, LANES),
    )
    if n_events != 2:
        gradient = lax.psum(gradient, "events")
    return (gradient.reshape(-1), correction.reshape(-1), weighted.reshape(-1))


def solution(mesh):
    every = P(("events", "shells"))
    placed = (P("shells"), P(("events", "shells"), None, None)) + (every,) * 6
    return jax.shard_map(
        functools.partial(local, mesh.shape["events"], mesh.shape["shells"]),
        mesh=mesh,
        in_specs=placed,
        out_specs=(P("shells"), P(), every),
        check_vma=False,
    )
```

```python
import functools

import jax
import jax.numpy as jnp
from jax import lax
from jax.experimental import pallas as pl
from jax.experimental.pallas import tpu as pltpu
from jax.sharding import PartitionSpec as P

PICK_BLK = 64
CELL_BLK = 128
STATIONS = 2048
LANES = 128
GROUP = 16
CHUNKS = 4
MESH = pl.DeviceIdType.MESH
F32 = jnp.float32
BF16 = jnp.bfloat16


def dot_nn(a, b):
    return lax.dot_general(a, b, (((1,), (0,)), ((), ())), preferred_element_type=F32)


def dot_nt(a, b):
    return lax.dot_general(a, b, (((1,), (1,)), ((), ())), preferred_element_type=F32)


def parts_of(x, count):
    parts = []
    for _ in range(count):
        part = x.astype(BF16)
        parts.append(part)
        x = x - part.astype(F32)
    return parts


def one_hot(rows, index_row):
    shape = (rows, index_row.shape[1])
    hit = lax.broadcasted_iota(jnp.int32, shape, 0) == index_row
    return jnp.where(hit, 1.0, 0.0).astype(BF16)


def diagonal_mask(j):
    row = lax.broadcasted_iota(jnp.int32, (GROUP, LANES), 0)
    lane = lax.broadcasted_iota(jnp.int32, (GROUP, LANES), 1)
    return row == 2 * j + lane // PICK_BLK


def swap_halves(x):
    return pltpu.roll(x, PICK_BLK, 1)


def finish_kernel(own_ref, other_ref, correction_in, weighted_in, gradient_ref, correction_ref, weighted_ref):
    gradient_ref[...] = own_ref[...].astype(F32) + other_ref[...].astype(F32)
    correction_ref[...] = correction_in[...]
    weighted_ref[...] = weighted_in[...]


def whole_kernel(
    n_events, n_shells,
    count_ref, blocks_ref, model_ref, pick_ref, cell_ref, observed_ref, weight_ref, station_ref,
    grads_out, grads_in, correction_ref, weighted_ref,
    blocks, pick_hot, pick_hot_t, cell_hot, model_rows, slot_rows, values, partial, landed,
    pair_in, paired, low_hot, spread, sums_out, sums_in, fitted, resid,
    load_sem, send_p, recv_p, send_a, recv_a, send_b, recv_b, send_c, recv_c, send_d, recv_d, send_e, recv_e,
):
    event = lax.axis_index("events")
    shell = lax.axis_index("shells")
    n_devices = n_events * n_shells
    mine = event * n_shells + shell
    rows = observed_ref.shape[0]
    n_high = sums_out.shape[0]
    slots = values.shape[0]
    cells = model_ref.shape[0]
    group_rows = partial.shape[0]
    per_chunk = slots // CHUNKS
    chunk_rows = per_chunk * PICK_BLK

    def after(x, i, n):
        return jnp.where(x + i >= n, x + i - n, x + i)

    def before(x, i, n):
        return jnp.where(x >= i, x - i, x + n - i)

    def load(c):
        part = pl.ds(pl.multiple_of(c * chunk_rows, chunk_rows), chunk_rows)
        return pltpu.make_async_copy(blocks_ref.at[part, :], blocks.at[part, :], load_sem.at[c])

    for c in range(CHUNKS):
        load(c).start()

    barrier = pltpu.get_barrier_semaphore()

    def greet_shell(i, carry):
        for j in range(n_events):
            pl.semaphore_signal(
                barrier, inc=1,
                device_id=(after(event, j, n_events), after(shell, i, n_shells)),
                device_id_type=MESH,
            )
        return carry

    for j in range(1, n_events):
        pl.semaphore_signal(
            barrier, inc=1, device_id=(after(event, j, n_events), shell), device_id_type=MESH
        )
    lax.fori_loop(1, n_shells, greet_shell, 0)

    alive = lax.broadcasted_iota(jnp.int32, (1, slots), 1) < count_ref[0]
    pick = jnp.where(alive, pick_ref[...], -2)
    cell = jnp.where(alive, cell_ref[...], -2)
    cell_column = jnp.transpose(jnp.broadcast_to(cell, (LANES, slots)))
    lane = lax.broadcasted_iota(jnp.int32, (slots, LANES), 1)
    found = jnp.zeros((slots, CELL_BLK), F32)
    for b in range(cells // LANES):
        hot = jnp.where(lane + b * LANES == cell_column, 1.0, 0.0).astype(BF16)
        found = found + dot_nn(hot, model_ref[b * LANES:(b + 1) * LANES, :])
    model_rows[...] = found.astype(BF16)
    pick_row = lax.shift_right_arithmetic(pick, 1)
    n_chips = n_shells // 2
    chip, core = shell // 2, lax.rem(shell, 2)
    half_rows = group_rows // 2
    owner = pick_row // rows
    moved = ((owner % 2) * n_chips + owner // 2) * rows + pick_row % rows
    pick_hot[...] = one_hot(group_rows, jnp.where(alive, moved, -1))
    cell_hot[...] = one_hot(cells, cell)
    pick_column = jnp.transpose(jnp.broadcast_to(pick, (LANES, slots)))
    half = (pick_column & 1) == lane // PICK_BLK
    pick_column = lax.shift_right_arithmetic(pick_column, 1)
    for b in range(group_rows // LANES):
        pick_hot_t[:, b * LANES:(b + 1) * LANES] = jnp.where(
            lane + b * LANES == pick_column, 1.0, 0.0
        ).astype(BF16)

    def forward_chunk(c, carry):
        load(c).wait()
        for g in range(per_chunk // GROUP):
            first = pl.multiple_of(c * per_chunk + g * GROUP, GROUP)
            block = blocks[pl.ds(pl.multiple_of(first * PICK_BLK, GROUP * PICK_BLK), GROUP * PICK_BLK), :]
            full = dot_nt(model_rows[pl.ds(first, GROUP), :], block)
            total = jnp.zeros((GROUP, LANES), F32)
            for j in range(GROUP // 2):
                total = total + jnp.where(diagonal_mask(j), full[:, j * LANES:(j + 1) * LANES], 0.0)
            values[pl.ds(first, GROUP), :] = total
        return carry

    lax.fori_loop(0, CHUNKS, forward_chunk, 0)
    v = values[...]
    v = jnp.where(half, v + swap_halves(v), 0.0)
    terms = jnp.concatenate(parts_of(v, 2), axis=1)

    def sum_half(which):
        piece = pl.ds(pl.multiple_of(which * half_rows, half_rows), half_rows)
        both = dot_nn(pick_hot[piece, :], terms)
        partial[piece, :] = both[:, :LANES] + both[:, LANES:]
        return piece

    sum_half_sent = sum_half(1 - core)
    pl.semaphore_wait(barrier, n_devices - 1)
    pair_copy = pltpu.make_async_remote_copy(
        src_ref=partial.at[sum_half_sent, :],
        dst_ref=pair_in,
        send_sem=send_p.at[0],
        recv_sem=recv_p.at[0],
        device_id=(event, shell + 1 - 2 * core),
        device_id_type=MESH,
    )
    pair_copy.start()
    kept = sum_half(core)
    pair_copy.wait_recv()
    paired[...] = partial[kept, :] + pair_in[...]

    def partial_copy(i, source):
        other = after(chip, i, n_chips)
        return pltpu.make_async_remote_copy(
            src_ref=paired.at[pl.ds(pl.multiple_of(other * rows, rows), rows), :],
            dst_ref=landed.at[source],
            send_sem=send_a.at[i],
            recv_sem=recv_a.at[source],
            device_id=(event, other * 2 + core),
            device_id_type=MESH,
        )

    def start_partial(i, carry):
        partial_copy(i, chip).start()
        return carry

    lax.fori_loop(1, n_chips, start_partial, 0)

    station = station_ref[...]
    high, low = station // LANES, lax.rem(station, LANES)
    for r in range(rows):
        low_hot[:, r * LANES:(r + 1) * LANES] = one_hot(LANES, low[r:r + 1, :])
    high_id = lax.broadcasted_iota(jnp.int32, (n_high, LANES), 0)

    def station_sums(x):
        pieces = parts_of(x, 3)
        for r in range(rows):
            hit = high_id == high[r:r + 1, :]
            for k in range(3):
                piece = pieces[k][r:r + 1, :].astype(F32)
                spread[k * n_high:(k + 1) * n_high, r * LANES:(r + 1) * LANES] = jnp.where(
                    hit, piece, 0.0
                ).astype(BF16)
        out = dot_nt(spread[...], low_hot[...])
        return out[:n_high] + (out[n_high:2 * n_high] + out[2 * n_high:])

    weight = weight_ref[...]
    denom = station_sums(weight)
    for h in range(n_high):
        sums_out[h, 1:2, :] = denom[h:h + 1, :]

    def take_partial(i, total):
        source = before(chip, i, n_chips)
        partial_copy(i, source).wait_recv()
        return total + landed[source]

    own = paired[pl.ds(pl.multiple_of(chip * rows, rows), rows), :]
    predicted = lax.fori_loop(1, n_chips, take_partial, own)
    misfit = observed_ref[...] - predicted
    numer = station_sums(weight * misfit)
    for h in range(n_high):
        sums_out[h, 0:1, :] = numer[h:h + 1, :]

    def sums_copy(i, j, source):
        other = after(shell, i, n_shells)
        return pltpu.make_async_remote_copy(
            src_ref=sums_out.at[other],
            dst_ref=sums_in.at[source],
            send_sem=send_b.at[i * n_events + j],
            recv_sem=recv_b.at[source],
            device_id=(after(event, j, n_events), other),
            device_id_type=MESH,
        )

    def sums_from(i, j):
        return before(event, j, n_events) * n_shells + before(shell, i, n_shells)

    def start_sums(i, carry):
        for j in range(n_events):
            sums_copy(i, j, mine).start()
        return carry

    def wait_sums(i, carry):
        for j in range(n_events):
            sums_copy(i, j, sums_from(i, j)).wait_recv()
        return carry

    for j in range(1, n_events):
        sums_copy(0, j, mine).start()
    lax.fori_loop(1, n_shells, start_sums, 0)
    sums_in[mine] = sums_out[shell]
    for j in range(1, n_events):
        sums_copy(0, j, sums_from(0, j)).wait_recv()
    lax.fori_loop(1, n_shells, wait_sums, 0)

    total = jnp.sum(sums_in[...], axis=0)
    fitted[shell] = total[0:1, :] / (total[1:2, :] + 1.0)

    def fitted_copy(i, source):
        return pltpu.make_async_remote_copy(
            src_ref=fitted.at[source],
            dst_ref=fitted.at[source],
            send_sem=send_c.at[i],
            recv_sem=recv_c.at[source],
            device_id=(event, after(shell, i, n_shells)),
            device_id_type=MESH,
        )

    def start_fitted(i, carry):
        fitted_copy(i, shell).start()
        return carry

    def wait_fitted(i, carry):
        fitted_copy(i, before(shell, i, n_shells)).wait_recv()
        return carry

    lax.fori_loop(1, n_shells, start_fitted, 0)
    lax.fori_loop(1, n_shells, wait_fitted, 0)

    correction = jnp.concatenate([fitted[h] for h in range(n_high)], axis=0)
    correction_ref[...] = correction[:correction_ref.shape[0]]
    pieces = jnp.concatenate(parts_of(correction, 3), axis=0)
    wide = dot_nn(pieces, low_hot[...])
    wide = wide[:n_high] + (wide[n_high:2 * n_high] + wide[2 * n_high:])
    picked = []
    for r in range(rows):
        hit = high_id == high[r:r + 1, :]
        picked.append(
            jnp.sum(jnp.where(hit, wide[:, r * LANES:(r + 1) * LANES], 0.0), axis=0, keepdims=True)
        )
    weighted = weight * (misfit - jnp.concatenate(picked, axis=0))
    weighted_ref[...] = weighted
    resid[shell] = weighted.astype(BF16)

    def resid_copy(i, source):
        return pltpu.make_async_remote_copy(
            src_ref=resid.at[source],
            dst_ref=resid.at[source],
            send_sem=send_d.at[i],
            recv_sem=recv_d.at[source],
            device_id=(event, after(shell, i, n_shells)),
            device_id_type=MESH,
        )

    def start_resid(i, carry):
        resid_copy(i, shell).start()
        return carry

    def wait_resid(i, carry):
        resid_copy(i, before(shell, i, n_shells)).wait_recv()
        return carry

    lax.fori_loop(1, n_shells, start_resid, 0)
    lax.fori_loop(1, n_shells, wait_resid, 0)

    found = dot_nn(pick_hot_t[...], resid[...].reshape(group_rows, LANES))
    found = jnp.where(half, found, 0.0)
    slot_rows[...] = found + swap_halves(found)

    def backward_chunk(c, carry):
        for g in range(per_chunk // GROUP):
            first = pl.multiple_of(c * per_chunk + g * GROUP, GROUP)
            picked = slot_rows[pl.ds(first, GROUP), :]
            wide = jnp.concatenate(
                [jnp.where(diagonal_mask(j), picked, 0.0).astype(BF16) for j in range(GROUP // 2)],
                axis=1,
            )
            block = blocks[pl.ds(pl.multiple_of(first * PICK_BLK, GROUP * PICK_BLK), GROUP * PICK_BLK), :]
            values[pl.ds(first, GROUP), :] = dot_nn(wide, block)
        return carry

    lax.fori_loop(0, CHUNKS, backward_chunk, 0)
    terms = jnp.concatenate(parts_of(values[...], 2), axis=1)
    part = cells // CHUNKS

    def grads_copy(c):
        piece = pl.ds(c * part, part)
        return pltpu.make_async_remote_copy(
            src_ref=grads_out.at[piece, :],
            dst_ref=grads_in.at[piece, :],
            send_sem=send_e.at[c],
            recv_sem=recv_e.at[c],
            device_id=(1 - event, shell),
            device_id_type=MESH,
        )

    for c in range(CHUNKS):
        both = dot_nn(cell_hot[c * part:(c + 1) * part, :], terms)
        grads = both[:, :LANES] + both[:, LANES:]
        if n_events == 2:
            grads_out[c * part:(c + 1) * part, :] = grads.astype(BF16)
            grads_copy(c).start()
        else:
            grads_out[c * part:(c + 1) * part, :] = grads

    def sent(i, carry):
        fitted_copy(i, shell).wait_send()
        resid_copy(i, shell).wait_send()
        for j in range(n_events):
            sums_copy(i, j, mine).wait_send()
        return carry

    for j in range(1, n_events):
        sums_copy(0, j, mine).wait_send()
    lax.fori_loop(1, n_shells, sent, 0)

    def partial_sent(i, carry):
        partial_copy(i, chip).wait_send()
        return carry

    pair_copy.wait_send()
    lax.fori_loop(1, n_chips, partial_sent, 0)
    if n_events == 2:
        for c in range(CHUNKS):
            grads_copy(c).wait()


def local(n_events, n_shells, model, sensitivity, pick_block, cell_block, blk_count, observed, pick_weight, station):
    slots = sensitivity.shape[0]
    cells = model.shape[0] // CELL_BLK
    rows = observed.shape[0] // LANES
    group_rows = rows * n_shells
    high_rows = STATIONS // LANES
    n_high = max(high_rows, n_shells)
    n_devices = n_events * n_shells
    n_chips = n_shells // 2
    two = n_events == 2
    dma = lambda n: pltpu.SemaphoreType.DMA((n,))
    vmem = pl.BlockSpec(memory_space=pltpu.VMEM)
    own, other, correction, weighted = pl.pallas_call(
        functools.partial(whole_kernel, n_events, n_shells),
        out_shape=(
            jax.ShapeDtypeStruct((cells, CELL_BLK), BF16 if two else F32),
            jax.ShapeDtypeStruct((cells if two else GROUP, CELL_BLK), BF16),
            jax.ShapeDtypeStruct((high_rows, LANES), F32),
            jax.ShapeDtypeStruct((rows, LANES), F32),
        ),
        in_specs=[pl.BlockSpec(memory_space=pltpu.SMEM), pl.BlockSpec(memory_space=pl.ANY)]
        + [vmem] * 6,
        out_specs=(vmem,) * 4,
        scratch_shapes=[
            pltpu.VMEM((slots * PICK_BLK, CELL_BLK), BF16),
            pltpu.VMEM((group_rows, slots), BF16),
            pltpu.VMEM((slots, group_rows), BF16),
            pltpu.VMEM((cells, slots), BF16),
            pltpu.VMEM((slots, CELL_BLK), BF16),
            pltpu.VMEM((slots, LANES), F32),
            pltpu.VMEM((slots, LANES), F32),
            pltpu.VMEM((group_rows, LANES), F32),
            pltpu.VMEM((n_chips, rows, LANES), F32),
            pltpu.VMEM((group_rows // 2, LANES), F32),
            pltpu.VMEM((group_rows // 2, LANES), F32),
            pltpu.VMEM((LANES, rows * LANES), BF16),
            pltpu.VMEM((3 * n_high, rows * LANES), BF16),
            pltpu.VMEM((n_high, 2, LANES), F32),
            pltpu.VMEM((n_devices, 2, LANES), F32),
            pltpu.VMEM((n_high, 1, LANES), F32),
            pltpu.VMEM((n_shells, rows, LANES), BF16),
            dma(CHUNKS), dma(1), dma(1),
            dma(n_chips), dma(n_chips), dma(n_devices), dma(n_devices),
            dma(n_shells), dma(n_shells), dma(n_shells), dma(n_shells),
            dma(CHUNKS), dma(CHUNKS),
        ],
        compiler_params=pltpu.CompilerParams(
            collective_id=0, has_side_effects=True, vmem_limit_bytes=60 * 1024 * 1024
        ),
    )(
        blk_count,
        sensitivity.reshape(slots * PICK_BLK, CELL_BLK),
        model.reshape(cells, CELL_BLK),
        pick_block.reshape(1, slots),
        cell_block.reshape(1, slots),
        observed.reshape(rows, LANES),
        pick_weight.reshape(rows, LANES),
        station.reshape(rows, LANES),
    )
    if two:
        gradient, correction, weighted = pl.pallas_call(
            finish_kernel,
            out_shape=(
                jax.ShapeDtypeStruct((cells, CELL_BLK), F32),
                jax.ShapeDtypeStruct((high_rows, LANES), F32),
                jax.ShapeDtypeStruct((rows, LANES), F32),
            ),
            in_specs=[vmem] * 4,
            out_specs=(vmem,) * 3,
            compiler_params=pltpu.CompilerParams(vmem_limit_bytes=60 * 1024 * 1024),
        )(own, other, correction, weighted)
    else:
        gradient = lax.psum(own, "events")
    return (gradient.reshape(-1), correction.reshape(-1), weighted.reshape(-1))


def solution(mesh):
    every = P(("events", "shells"))
    placed = (P("shells"), P(("events", "shells"), None, None)) + (every,) * 6
    return jax.shard_map(
        functools.partial(local, mesh.shape["events"], mesh.shape["shells"]),
        mesh=mesh,
        in_specs=placed,
        out_specs=(P("shells"), P(), every),
        check_vma=False,
    )
```

```python
import functools

import jax
import jax.numpy as jnp
from jax import lax
from jax.experimental import pallas as pl
from jax.experimental.pallas import tpu as pltpu
from jax.sharding import PartitionSpec as P

PICK_BLK = 64
CELL_BLK = 128
STATIONS = 2048
LANES = 128
GROUP = 16
CHUNKS = 4
MESH = pl.DeviceIdType.MESH
F32 = jnp.float32
BF16 = jnp.bfloat16


def dot_nn(a, b):
    return lax.dot_general(a, b, (((1,), (0,)), ((), ())), preferred_element_type=F32)


def dot_nt(a, b):
    return lax.dot_general(a, b, (((1,), (1,)), ((), ())), preferred_element_type=F32)


def parts_of(x, count):
    parts = []
    for _ in range(count):
        part = x.astype(BF16)
        parts.append(part)
        x = x - part.astype(F32)
    return parts


def one_hot(rows, index_row):
    shape = (rows, index_row.shape[1])
    hit = lax.broadcasted_iota(jnp.int32, shape, 0) == index_row
    return jnp.where(hit, 1.0, 0.0).astype(BF16)


def diagonal_mask(j):
    row = lax.broadcasted_iota(jnp.int32, (GROUP, LANES), 0)
    lane = lax.broadcasted_iota(jnp.int32, (GROUP, LANES), 1)
    return row == 2 * j + lane // PICK_BLK


def swap_halves(x):
    return pltpu.roll(x, PICK_BLK, 1)


def finish_kernel(own_ref, other_ref, correction_in, weighted_in, gradient_ref, correction_ref, weighted_ref):
    gradient_ref[...] = own_ref[...].astype(F32) + other_ref[...].astype(F32)
    correction_ref[...] = correction_in[...]
    weighted_ref[...] = weighted_in[...]


def whole_kernel(
    n_events, n_shells,
    count_ref, blocks_ref, model_ref, pick_ref, cell_ref, observed_ref, weight_ref, station_ref,
    grads_out, grads_in, correction_ref, weighted_ref,
    blocks, pick_hot, pick_hot_t, cell_hot, model_rows, slot_rows, values, partial, landed,
    pair_in, paired, low_hot, spread, sums_out, sums_in, fitted, resid,
    load_sem, send_p, recv_p, send_a, recv_a, send_b, recv_b, send_c, recv_c, send_d, recv_d, send_f, recv_f, send_e, recv_e,
):
    event = lax.axis_index("events")
    shell = lax.axis_index("shells")
    n_devices = n_events * n_shells
    mine = event * n_shells + shell
    rows = observed_ref.shape[0]
    n_high = sums_out.shape[0]
    slots = values.shape[0]
    cells = model_ref.shape[0]
    group_rows = partial.shape[0]
    per_chunk = slots // CHUNKS
    chunk_rows = per_chunk * PICK_BLK

    def after(x, i, n):
        return jnp.where(x + i >= n, x + i - n, x + i)

    def before(x, i, n):
        return jnp.where(x >= i, x - i, x + n - i)

    def load(c):
        part = pl.ds(pl.multiple_of(c * chunk_rows, chunk_rows), chunk_rows)
        return pltpu.make_async_copy(blocks_ref.at[part, :], blocks.at[part, :], load_sem.at[c])

    for c in range(CHUNKS):
        load(c).start()

    barrier = pltpu.get_barrier_semaphore()

    def greet_shell(i, carry):
        for j in range(n_events):
            pl.semaphore_signal(
                barrier, inc=1,
                device_id=(after(event, j, n_events), after(shell, i, n_shells)),
                device_id_type=MESH,
            )
        return carry

    for j in range(1, n_events):
        pl.semaphore_signal(
            barrier, inc=1, device_id=(after(event, j, n_events), shell), device_id_type=MESH
        )
    lax.fori_loop(1, n_shells, greet_shell, 0)

    alive = lax.broadcasted_iota(jnp.int32, (1, slots), 1) < count_ref[0]
    pick = jnp.where(alive, pick_ref[...], -2)
    cell = jnp.where(alive, cell_ref[...], -2)
    cell_column = jnp.transpose(jnp.broadcast_to(cell, (LANES, slots)))
    lane = lax.broadcasted_iota(jnp.int32, (slots, LANES), 1)
    found = jnp.zeros((slots, CELL_BLK), F32)
    for b in range(cells // LANES):
        hot = jnp.where(lane + b * LANES == cell_column, 1.0, 0.0).astype(BF16)
        found = found + dot_nn(hot, model_ref[b * LANES:(b + 1) * LANES, :])
    model_rows[...] = found.astype(BF16)
    pick_row = lax.shift_right_arithmetic(pick, 1)
    n_chips = n_shells // 2
    chip, core = shell // 2, lax.rem(shell, 2)
    half_rows = group_rows // 2
    owner = pick_row // rows
    moved = ((owner % 2) * n_chips + owner // 2) * rows + pick_row % rows
    pick_hot[...] = one_hot(group_rows, jnp.where(alive, moved, -1))
    cell_hot[...] = one_hot(cells, cell)
    pick_column = jnp.transpose(jnp.broadcast_to(pick, (LANES, slots)))
    half = (pick_column & 1) == lane // PICK_BLK
    pick_column = lax.shift_right_arithmetic(pick_column, 1)
    for b in range(group_rows // LANES):
        pick_hot_t[:, b * LANES:(b + 1) * LANES] = jnp.where(
            lane + b * LANES == pick_column, 1.0, 0.0
        ).astype(BF16)

    def forward_chunk(c, carry):
        load(c).wait()
        for g in range(per_chunk // GROUP):
            first = pl.multiple_of(c * per_chunk + g * GROUP, GROUP)
            block = blocks[pl.ds(pl.multiple_of(first * PICK_BLK, GROUP * PICK_BLK), GROUP * PICK_BLK), :]
            full = dot_nt(model_rows[pl.ds(first, GROUP), :], block)
            total = jnp.zeros((GROUP, LANES), F32)
            for j in range(GROUP // 2):
                total = total + jnp.where(diagonal_mask(j), full[:, j * LANES:(j + 1) * LANES], 0.0)
            values[pl.ds(first, GROUP), :] = total
        return carry

    lax.fori_loop(0, CHUNKS, forward_chunk, 0)
    v = values[...]
    v = jnp.where(half, v + swap_halves(v), 0.0)
    terms = jnp.concatenate(parts_of(v, 2), axis=1)

    def sum_half(which):
        piece = pl.ds(pl.multiple_of(which * half_rows, half_rows), half_rows)
        both = dot_nn(pick_hot[piece, :], terms)
        partial[piece, :] = both[:, :LANES] + both[:, LANES:]
        return piece

    sum_half_sent = sum_half(1 - core)
    pl.semaphore_wait(barrier, n_devices - 1)
    pair_copy = pltpu.make_async_remote_copy(
        src_ref=partial.at[sum_half_sent, :],
        dst_ref=pair_in,
        send_sem=send_p.at[0],
        recv_sem=recv_p.at[0],
        device_id=(event, shell + 1 - 2 * core),
        device_id_type=MESH,
    )
    pair_copy.start()
    kept = sum_half(core)
    pair_copy.wait_recv()
    paired[...] = partial[kept, :] + pair_in[...]

    def partial_copy(i, source):
        other = after(chip, i, n_chips)
        return pltpu.make_async_remote_copy(
            src_ref=paired.at[pl.ds(pl.multiple_of(other * rows, rows), rows), :],
            dst_ref=landed.at[source],
            send_sem=send_a.at[i],
            recv_sem=recv_a.at[source],
            device_id=(event, other * 2 + core),
            device_id_type=MESH,
        )

    def start_partial(i, carry):
        partial_copy(i, chip).start()
        return carry

    lax.fori_loop(1, n_chips, start_partial, 0)

    station = station_ref[...]
    high, low = station // LANES, lax.rem(station, LANES)
    for r in range(rows):
        low_hot[:, r * LANES:(r + 1) * LANES] = one_hot(LANES, low[r:r + 1, :])
    high_id = lax.broadcasted_iota(jnp.int32, (n_high, LANES), 0)

    def station_sums(x):
        pieces = parts_of(x, 2)
        for r in range(rows):
            hit = high_id == high[r:r + 1, :]
            for k in range(2):
                piece = pieces[k][r:r + 1, :].astype(F32)
                spread[k * n_high:(k + 1) * n_high, r * LANES:(r + 1) * LANES] = jnp.where(
                    hit, piece, 0.0
                ).astype(BF16)
        out = dot_nt(spread[...], low_hot[...])
        return out[:n_high] + out[n_high:]

    weight = weight_ref[...]
    denom = station_sums(weight)
    for h in range(n_high):
        sums_out[h, 1:2, :] = denom[h:h + 1, :]

    def take_partial(i, total):
        source = before(chip, i, n_chips)
        partial_copy(i, source).wait_recv()
        return total + landed[source]

    own = paired[pl.ds(pl.multiple_of(chip * rows, rows), rows), :]
    predicted = lax.fori_loop(1, n_chips, take_partial, own)
    misfit = observed_ref[...] - predicted
    numer = station_sums(weight * misfit)
    for h in range(n_high):
        sums_out[h, 0:1, :] = numer[h:h + 1, :]

    def sums_copy(i, j, source):
        other = after(shell, i, n_shells)
        return pltpu.make_async_remote_copy(
            src_ref=sums_out.at[other],
            dst_ref=sums_in.at[source],
            send_sem=send_b.at[i * n_events + j],
            recv_sem=recv_b.at[source],
            device_id=(after(event, j, n_events), other),
            device_id_type=MESH,
        )

    def sums_from(i, j):
        return before(event, j, n_events) * n_shells + before(shell, i, n_shells)

    def start_sums(i, carry):
        for j in range(n_events):
            sums_copy(i, j, mine).start()
        return carry

    def wait_sums(i, carry):
        for j in range(n_events):
            sums_copy(i, j, sums_from(i, j)).wait_recv()
        return carry

    for j in range(1, n_events):
        sums_copy(0, j, mine).start()
    lax.fori_loop(1, n_shells, start_sums, 0)
    sums_in[mine] = sums_out[shell]
    for j in range(1, n_events):
        sums_copy(0, j, sums_from(0, j)).wait_recv()
    lax.fori_loop(1, n_shells, wait_sums, 0)

    total = jnp.sum(sums_in[...], axis=0)
    fitted[shell] = total[0:1, :] / (total[1:2, :] + 1.0)

    def fitted_copy(i, source):
        return pltpu.make_async_remote_copy(
            src_ref=fitted.at[source],
            dst_ref=fitted.at[source],
            send_sem=send_c.at[i],
            recv_sem=recv_c.at[source],
            device_id=(event, after(shell, i, n_shells)),
            device_id_type=MESH,
        )

    def start_fitted(i, carry):
        fitted_copy(i, shell).start()
        return carry

    def wait_fitted(i, carry):
        fitted_copy(i, before(shell, i, n_shells)).wait_recv()
        return carry

    lax.fori_loop(1, n_shells, start_fitted, 0)
    lax.fori_loop(1, n_shells, wait_fitted, 0)

    correction = jnp.concatenate([fitted[h] for h in range(n_high)], axis=0)
    correction_ref[...] = correction[:correction_ref.shape[0]]
    pieces = jnp.concatenate(parts_of(correction, 2), axis=0)
    wide = dot_nn(pieces, low_hot[...])
    wide = wide[:n_high] + wide[n_high:]
    picked = []
    for r in range(rows):
        hit = high_id == high[r:r + 1, :]
        picked.append(
            jnp.sum(jnp.where(hit, wide[:, r * LANES:(r + 1) * LANES], 0.0), axis=0, keepdims=True)
        )
    weighted = weight * (misfit - jnp.concatenate(picked, axis=0))
    weighted_ref[...] = weighted
    resid[shell] = weighted.astype(BF16)

    def resid_copy(i, source):
        return pltpu.make_async_remote_copy(
            src_ref=resid.at[source],
            dst_ref=resid.at[source],
            send_sem=send_d.at[i],
            recv_sem=recv_d.at[i],
            device_id=(event, after(chip, i, n_chips) * 2 + core),
            device_id_type=MESH,
        )

    def shared_copy(i, source):
        return pltpu.make_async_remote_copy(
            src_ref=resid.at[source],
            dst_ref=resid.at[source],
            send_sem=send_f.at[i],
            recv_sem=recv_f.at[i],
            device_id=(event, shell + 1 - 2 * core),
            device_id_type=MESH,
        )

    def start_resid(i, carry):
        resid_copy(i, shell).start()
        return carry

    def share_resid(i, carry):
        source = before(chip, i, n_chips) * 2 + core
        resid_copy(i, source).wait_recv()
        shared_copy(i, source).start()
        return carry

    def wait_resid(i, carry):
        shared_copy(i, before(chip, i, n_chips) * 2 + 1 - core).wait_recv()
        return carry

    lax.fori_loop(1, n_chips, start_resid, 0)
    shared_copy(0, shell).start()
    lax.fori_loop(1, n_chips, share_resid, 0)
    lax.fori_loop(0, n_chips, wait_resid, 0)

    found = dot_nn(pick_hot_t[...], resid[...].reshape(group_rows, LANES))
    found = jnp.where(half, found, 0.0)
    slot_rows[...] = found + swap_halves(found)

    def backward_chunk(c, carry):
        for g in range(per_chunk // GROUP):
            first = pl.multiple_of(c * per_chunk + g * GROUP, GROUP)
            picked = slot_rows[pl.ds(first, GROUP), :]
            wide = jnp.concatenate(
                [jnp.where(diagonal_mask(j), picked, 0.0).astype(BF16) for j in range(GROUP // 2)],
                axis=1,
            )
            block = blocks[pl.ds(pl.multiple_of(first * PICK_BLK, GROUP * PICK_BLK), GROUP * PICK_BLK), :]
            values[pl.ds(first, GROUP), :] = dot_nn(wide, block)
        return carry

    lax.fori_loop(0, CHUNKS, backward_chunk, 0)
    terms = jnp.concatenate(parts_of(values[...], 2), axis=1)
    part = cells // CHUNKS

    def grads_copy(c):
        piece = pl.ds(c * part, part)
        return pltpu.make_async_remote_copy(
            src_ref=grads_out.at[piece, :],
            dst_ref=grads_in.at[piece, :],
            send_sem=send_e.at[c],
            recv_sem=recv_e.at[c],
            device_id=(1 - event, shell),
            device_id_type=MESH,
        )

    for c in range(CHUNKS):
        both = dot_nn(cell_hot[c * part:(c + 1) * part, :], terms)
        grads = both[:, :LANES] + both[:, LANES:]
        if n_events == 2:
            grads_out[c * part:(c + 1) * part, :] = grads.astype(BF16)
            grads_copy(c).start()
        else:
            grads_out[c * part:(c + 1) * part, :] = grads

    def sent(i, carry):
        fitted_copy(i, shell).wait_send()
        for j in range(n_events):
            sums_copy(i, j, mine).wait_send()
        return carry

    for j in range(1, n_events):
        sums_copy(0, j, mine).wait_send()
    lax.fori_loop(1, n_shells, sent, 0)

    def partial_sent(i, carry):
        partial_copy(i, chip).wait_send()
        resid_copy(i, shell).wait_send()
        shared_copy(i, before(chip, i, n_chips) * 2 + core).wait_send()
        return carry

    pair_copy.wait_send()
    shared_copy(0, shell).wait_send()
    lax.fori_loop(1, n_chips, partial_sent, 0)
    if n_events == 2:
        for c in range(CHUNKS):
            grads_copy(c).wait()


def local(n_events, n_shells, model, sensitivity, pick_block, cell_block, blk_count, observed, pick_weight, station):
    slots = sensitivity.shape[0]
    cells = model.shape[0] // CELL_BLK
    rows = observed.shape[0] // LANES
    group_rows = rows * n_shells
    high_rows = STATIONS // LANES
    n_high = max(high_rows, n_shells)
    n_devices = n_events * n_shells
    n_chips = n_shells // 2
    two = n_events == 2
    dma = lambda n: pltpu.SemaphoreType.DMA((n,))
    vmem = pl.BlockSpec(memory_space=pltpu.VMEM)
    own, other, correction, weighted = pl.pallas_call(
        functools.partial(whole_kernel, n_events, n_shells),
        out_shape=(
            jax.ShapeDtypeStruct((cells, CELL_BLK), BF16 if two else F32),
            jax.ShapeDtypeStruct((cells if two else GROUP, CELL_BLK), BF16),
            jax.ShapeDtypeStruct((high_rows, LANES), F32),
            jax.ShapeDtypeStruct((rows, LANES), F32),
        ),
        in_specs=[pl.BlockSpec(memory_space=pltpu.SMEM), pl.BlockSpec(memory_space=pl.ANY)]
        + [vmem] * 6,
        out_specs=(vmem,) * 4,
        scratch_shapes=[
            pltpu.VMEM((slots * PICK_BLK, CELL_BLK), BF16),
            pltpu.VMEM((group_rows, slots), BF16),
            pltpu.VMEM((slots, group_rows), BF16),
            pltpu.VMEM((cells, slots), BF16),
            pltpu.VMEM((slots, CELL_BLK), BF16),
            pltpu.VMEM((slots, LANES), F32),
            pltpu.VMEM((slots, LANES), F32),
            pltpu.VMEM((group_rows, LANES), F32),
            pltpu.VMEM((n_chips, rows, LANES), F32),
            pltpu.VMEM((group_rows // 2, LANES), F32),
            pltpu.VMEM((group_rows // 2, LANES), F32),
            pltpu.VMEM((LANES, rows * LANES), BF16),
            pltpu.VMEM((2 * n_high, rows * LANES), BF16),
            pltpu.VMEM((n_high, 2, LANES), F32),
            pltpu.VMEM((n_devices, 2, LANES), F32),
            pltpu.VMEM((n_high, 1, LANES), F32),
            pltpu.VMEM((n_shells, rows, LANES), BF16),
            dma(CHUNKS), dma(1), dma(1),
            dma(n_chips), dma(n_chips), dma(n_devices), dma(n_devices),
            dma(n_shells), dma(n_shells), dma(n_chips), dma(n_chips), dma(n_chips), dma(n_chips),
            dma(CHUNKS), dma(CHUNKS),
        ],
        compiler_params=pltpu.CompilerParams(
            collective_id=0, has_side_effects=True, vmem_limit_bytes=60 * 1024 * 1024
        ),
    )(
        blk_count,
        sensitivity.reshape(slots * PICK_BLK, CELL_BLK),
        model.reshape(cells, CELL_BLK),
        pick_block.reshape(1, slots),
        cell_block.reshape(1, slots),
        observed.reshape(rows, LANES),
        pick_weight.reshape(rows, LANES),
        station.reshape(rows, LANES),
    )
    if two:
        gradient, correction, weighted = pl.pallas_call(
            finish_kernel,
            out_shape=(
                jax.ShapeDtypeStruct((cells, CELL_BLK), F32),
                jax.ShapeDtypeStruct((high_rows, LANES), F32),
                jax.ShapeDtypeStruct((rows, LANES), F32),
            ),
            in_specs=[vmem] * 4,
            out_specs=(vmem,) * 3,
            compiler_params=pltpu.CompilerParams(vmem_limit_bytes=60 * 1024 * 1024),
        )(own, other, correction, weighted)
    else:
        gradient = lax.psum(own, "events")
    return (gradient.reshape(-1), correction.reshape(-1), weighted.reshape(-1))


def solution(mesh):
    every = P(("events", "shells"))
    placed = (P("shells"), P(("events", "shells"), None, None)) + (every,) * 6
    return jax.shard_map(
        functools.partial(local, mesh.shape["events"], mesh.shape["shells"]),
        mesh=mesh,
        in_specs=placed,
        out_specs=(P("shells"), P(), every),
        check_vma=False,
    )
```

```python
import functools

import jax
import jax.numpy as jnp
from jax import lax
from jax.experimental import pallas as pl
from jax.experimental.pallas import tpu as pltpu
from jax.sharding import PartitionSpec as P

PICK_BLK = 64
CELL_BLK = 128
STATIONS = 2048
LANES = 128
GROUP = 16
CHUNKS = 4
MESH = pl.DeviceIdType.MESH
F32 = jnp.float32
BF16 = jnp.bfloat16


def dot_nn(a, b):
    return lax.dot_general(a, b, (((1,), (0,)), ((), ())), preferred_element_type=F32)


def dot_nt(a, b):
    return lax.dot_general(a, b, (((1,), (1,)), ((), ())), preferred_element_type=F32)


def parts_of(x, count):
    parts = []
    for _ in range(count):
        part = x.astype(BF16)
        parts.append(part)
        x = x - part.astype(F32)
    return parts


def one_hot(rows, index_row):
    shape = (rows, index_row.shape[1])
    hit = lax.broadcasted_iota(jnp.int32, shape, 0) == index_row
    return jnp.where(hit, 1.0, 0.0).astype(BF16)


def diagonal_mask(j):
    row = lax.broadcasted_iota(jnp.int32, (GROUP, LANES), 0)
    lane = lax.broadcasted_iota(jnp.int32, (GROUP, LANES), 1)
    return row == 2 * j + lane // PICK_BLK


def swap_halves(x):
    return pltpu.roll(x, PICK_BLK, 1)


def finish_kernel(own_ref, other_ref, correction_in, weighted_in, gradient_ref, correction_ref, weighted_ref):
    gradient_ref[...] = own_ref[...].astype(F32) + other_ref[...].astype(F32)
    correction_ref[...] = correction_in[...]
    weighted_ref[...] = weighted_in[...]


def whole_kernel(
    n_events, n_shells,
    count_ref, blocks_ref, model_ref, pick_ref, cell_ref, observed_ref, weight_ref, station_ref,
    grads_out, grads_in, correction_ref, weighted_ref,
    blocks, pick_hot, pick_hot_t, cell_hot, model_rows, slot_rows, values, partial, landed,
    pair_in, paired, low_hot, spread, sums_out, sums_in, fitted, resid,
    load_sem, send_p, recv_p, send_a, recv_a, send_b, recv_b, send_c, recv_c, send_d, recv_d, send_e, recv_e,
):
    event = lax.axis_index("events")
    shell = lax.axis_index("shells")
    n_devices = n_events * n_shells
    mine = event * n_shells + shell
    rows = observed_ref.shape[0]
    n_high = sums_out.shape[0]
    slots = values.shape[0]
    cells = model_ref.shape[0]
    group_rows = partial.shape[0]
    per_chunk = slots // CHUNKS
    chunk_rows = per_chunk * PICK_BLK

    def after(x, i, n):
        return jnp.where(x + i >= n, x + i - n, x + i)

    def before(x, i, n):
        return jnp.where(x >= i, x - i, x + n - i)

    def load(c):
        part = pl.ds(pl.multiple_of(c * chunk_rows, chunk_rows), chunk_rows)
        return pltpu.make_async_copy(blocks_ref.at[part, :], blocks.at[part, :], load_sem.at[c])

    for c in range(CHUNKS):
        load(c).start()

    barrier = pltpu.get_barrier_semaphore()

    def greet_shell(i, carry):
        for j in range(n_events):
            pl.semaphore_signal(
                barrier, inc=1,
                device_id=(after(event, j, n_events), after(shell, i, n_shells)),
                device_id_type=MESH,
            )
        return carry

    for j in range(1, n_events):
        pl.semaphore_signal(
            barrier, inc=1, device_id=(after(event, j, n_events), shell), device_id_type=MESH
        )
    lax.fori_loop(1, n_shells, greet_shell, 0)

    alive = lax.broadcasted_iota(jnp.int32, (1, slots), 1) < count_ref[0]
    pick = jnp.where(alive, pick_ref[...], -2)
    cell = jnp.where(alive, cell_ref[...], -2)
    cell_column = jnp.transpose(jnp.broadcast_to(cell, (LANES, slots)))
    lane = lax.broadcasted_iota(jnp.int32, (slots, LANES), 1)
    found = jnp.zeros((slots, CELL_BLK), F32)
    for b in range(cells // LANES):
        hot = jnp.where(lane + b * LANES == cell_column, 1.0, 0.0).astype(BF16)
        found = found + dot_nn(hot, model_ref[b * LANES:(b + 1) * LANES, :])
    model_rows[...] = found.astype(BF16)
    pick_row = lax.shift_right_arithmetic(pick, 1)
    n_chips = n_shells // 2
    chip, core = shell // 2, lax.rem(shell, 2)
    half_rows = group_rows // 2
    owner = pick_row // rows
    moved = ((owner % 2) * n_chips + owner // 2) * rows + pick_row % rows
    pick_hot[...] = one_hot(group_rows, jnp.where(alive, moved, -1))
    pick_column = jnp.transpose(jnp.broadcast_to(pick, (LANES, slots)))
    half = (pick_column & 1) == lane // PICK_BLK
    pick_column = lax.shift_right_arithmetic(pick_column, 1)
    for b in range(group_rows // LANES):
        pick_hot_t[:, b * LANES:(b + 1) * LANES] = jnp.where(
            lane + b * LANES == pick_column, 1.0, 0.0
        ).astype(BF16)

    def forward_chunk(c, carry):
        load(c).wait()
        for g in range(per_chunk // GROUP):
            first = pl.multiple_of(c * per_chunk + g * GROUP, GROUP)
            block = blocks[pl.ds(pl.multiple_of(first * PICK_BLK, GROUP * PICK_BLK), GROUP * PICK_BLK), :]
            full = dot_nt(model_rows[pl.ds(first, GROUP), :], block)
            total = jnp.zeros((GROUP, LANES), F32)
            for j in range(GROUP // 2):
                total = total + jnp.where(diagonal_mask(j), full[:, j * LANES:(j + 1) * LANES], 0.0)
            values[pl.ds(first, GROUP), :] = total
        return carry

    lax.fori_loop(0, CHUNKS, forward_chunk, 0)
    v = values[...]
    v = jnp.where(half, v + swap_halves(v), 0.0)
    terms = jnp.concatenate(parts_of(v, 2), axis=1)

    def sum_half(which):
        piece = pl.ds(pl.multiple_of(which * half_rows, half_rows), half_rows)
        both = dot_nn(pick_hot[piece, :], terms)
        partial[piece, :] = both[:, :LANES] + both[:, LANES:]
        return piece

    sum_half_sent = sum_half(1 - core)
    pl.semaphore_wait(barrier, n_devices - 1)
    pair_copy = pltpu.make_async_remote_copy(
        src_ref=partial.at[sum_half_sent, :],
        dst_ref=pair_in,
        send_sem=send_p.at[0],
        recv_sem=recv_p.at[0],
        device_id=(event, shell + 1 - 2 * core),
        device_id_type=MESH,
    )
    pair_copy.start()
    kept = sum_half(core)
    pair_copy.wait_recv()
    paired[...] = partial[kept, :] + pair_in[...]

    def partial_copy(i, source):
        other = after(chip, i, n_chips)
        return pltpu.make_async_remote_copy(
            src_ref=paired.at[pl.ds(pl.multiple_of(other * rows, rows), rows), :],
            dst_ref=landed.at[source],
            send_sem=send_a.at[i],
            recv_sem=recv_a.at[source],
            device_id=(event, other * 2 + core),
            device_id_type=MESH,
        )

    def start_partial(i, carry):
        partial_copy(i, chip).start()
        return carry

    lax.fori_loop(1, n_chips, start_partial, 0)

    station = station_ref[...]
    high, low = station // LANES, lax.rem(station, LANES)
    for r in range(rows):
        low_hot[:, r * LANES:(r + 1) * LANES] = one_hot(LANES, low[r:r + 1, :])
    high_id = lax.broadcasted_iota(jnp.int32, (n_high, LANES), 0)

    def station_sums(x):
        pieces = parts_of(x, 2)
        for r in range(rows):
            hit = high_id == high[r:r + 1, :]
            for k in range(2):
                piece = pieces[k][r:r + 1, :].astype(F32)
                spread[k * n_high:(k + 1) * n_high, r * LANES:(r + 1) * LANES] = jnp.where(
                    hit, piece, 0.0
                ).astype(BF16)
        out = dot_nt(spread[...], low_hot[...])
        return out[:n_high] + out[n_high:]

    weight = weight_ref[...]
    denom = station_sums(weight)
    for h in range(n_high):
        sums_out[h, 1:2, :] = denom[h:h + 1, :]

    def take_partial(i, total):
        source = before(chip, i, n_chips)
        partial_copy(i, source).wait_recv()
        return total + landed[source]

    own = paired[pl.ds(pl.multiple_of(chip * rows, rows), rows), :]
    predicted = lax.fori_loop(1, n_chips, take_partial, own)
    misfit = observed_ref[...] - predicted
    numer = station_sums(weight * misfit)
    for h in range(n_high):
        sums_out[h, 0:1, :] = numer[h:h + 1, :]

    def sums_copy(i, j, source):
        other = after(shell, i, n_shells)
        return pltpu.make_async_remote_copy(
            src_ref=sums_out.at[other],
            dst_ref=sums_in.at[source],
            send_sem=send_b.at[i * n_events + j],
            recv_sem=recv_b.at[source],
            device_id=(after(event, j, n_events), other),
            device_id_type=MESH,
        )

    def sums_from(i, j):
        return before(event, j, n_events) * n_shells + before(shell, i, n_shells)

    def start_sums(i, carry):
        for j in range(n_events):
            sums_copy(i, j, mine).start()
        return carry

    def wait_sums(i, carry):
        for j in range(n_events):
            sums_copy(i, j, sums_from(i, j)).wait_recv()
        return carry

    for j in range(1, n_events):
        sums_copy(0, j, mine).start()
    lax.fori_loop(1, n_shells, start_sums, 0)
    sums_in[mine] = sums_out[shell]
    for j in range(1, n_events):
        sums_copy(0, j, sums_from(0, j)).wait_recv()
    lax.fori_loop(1, n_shells, wait_sums, 0)

    total = jnp.sum(sums_in[...], axis=0)
    fitted[shell] = total[0:1, :] / (total[1:2, :] + 1.0)

    def fitted_copy(i, source):
        return pltpu.make_async_remote_copy(
            src_ref=fitted.at[source],
            dst_ref=fitted.at[source],
            send_sem=send_c.at[i],
            recv_sem=recv_c.at[source],
            device_id=(event, after(shell, i, n_shells)),
            device_id_type=MESH,
        )

    def start_fitted(i, carry):
        fitted_copy(i, shell).start()
        return carry

    def wait_fitted(i, carry):
        fitted_copy(i, before(shell, i, n_shells)).wait_recv()
        return carry

    lax.fori_loop(1, n_shells, start_fitted, 0)
    lax.fori_loop(1, n_shells, wait_fitted, 0)

    correction = jnp.concatenate([fitted[h] for h in range(n_high)], axis=0)
    correction_ref[...] = correction[:correction_ref.shape[0]]
    pieces = jnp.concatenate(parts_of(correction, 2), axis=0)
    wide = dot_nn(pieces, low_hot[...])
    wide = wide[:n_high] + wide[n_high:]
    picked = []
    for r in range(rows):
        hit = high_id == high[r:r + 1, :]
        picked.append(
            jnp.sum(jnp.where(hit, wide[:, r * LANES:(r + 1) * LANES], 0.0), axis=0, keepdims=True)
        )
    weighted = weight * (misfit - jnp.concatenate(picked, axis=0))
    weighted_ref[...] = weighted
    resid[shell] = weighted.astype(BF16)

    def resid_copy(i, source):
        return pltpu.make_async_remote_copy(
            src_ref=resid.at[source],
            dst_ref=resid.at[source],
            send_sem=send_d.at[i],
            recv_sem=recv_d.at[source],
            device_id=(event, after(shell, i, n_shells)),
            device_id_type=MESH,
        )

    def start_resid(i, carry):
        resid_copy(i, shell).start()
        return carry

    def wait_resid(i, carry):
        resid_copy(i, before(shell, i, n_shells)).wait_recv()
        return carry

    lax.fori_loop(1, n_shells, start_resid, 0)
    cell_hot[...] = one_hot(cells, cell)
    lax.fori_loop(1, n_shells, wait_resid, 0)

    found = dot_nn(pick_hot_t[...], resid[...].reshape(group_rows, LANES))
    found = jnp.where(half, found, 0.0)
    slot_rows[...] = found + swap_halves(found)

    def backward_chunk(c, carry):
        for g in range(per_chunk // GROUP):
            first = pl.multiple_of(c * per_chunk + g * GROUP, GROUP)
            picked = slot_rows[pl.ds(first, GROUP), :]
            wide = jnp.concatenate(
                [jnp.where(diagonal_mask(j), picked, 0.0).astype(BF16) for j in range(GROUP // 2)],
                axis=1,
            )
            block = blocks[pl.ds(pl.multiple_of(first * PICK_BLK, GROUP * PICK_BLK), GROUP * PICK_BLK), :]
            values[pl.ds(first, GROUP), :] = dot_nn(wide, block)
        return carry

    lax.fori_loop(0, CHUNKS, backward_chunk, 0)
    terms = jnp.concatenate(parts_of(values[...], 2), axis=1)
    part = cells // CHUNKS

    def grads_copy(c):
        piece = pl.ds(c * part, part)
        return pltpu.make_async_remote_copy(
            src_ref=grads_out.at[piece, :],
            dst_ref=grads_in.at[piece, :],
            send_sem=send_e.at[c],
            recv_sem=recv_e.at[c],
            device_id=(1 - event, shell),
            device_id_type=MESH,
        )

    for c in range(CHUNKS):
        both = dot_nn(cell_hot[c * part:(c + 1) * part, :], terms)
        grads = both[:, :LANES] + both[:, LANES:]
        if n_events == 2:
            grads_out[c * part:(c + 1) * part, :] = grads.astype(BF16)
            grads_copy(c).start()
        else:
            grads_out[c * part:(c + 1) * part, :] = grads

    def sent(i, carry):
        fitted_copy(i, shell).wait_send()
        resid_copy(i, shell).wait_send()
        for j in range(n_events):
            sums_copy(i, j, mine).wait_send()
        return carry

    for j in range(1, n_events):
        sums_copy(0, j, mine).wait_send()
    lax.fori_loop(1, n_shells, sent, 0)

    def partial_sent(i, carry):
        partial_copy(i, chip).wait_send()
        return carry

    pair_copy.wait_send()
    lax.fori_loop(1, n_chips, partial_sent, 0)
    if n_events == 2:
        for c in range(CHUNKS):
            grads_copy(c).wait()


def local(n_events, n_shells, model, sensitivity, pick_block, cell_block, blk_count, observed, pick_weight, station):
    slots = sensitivity.shape[0]
    cells = model.shape[0] // CELL_BLK
    rows = observed.shape[0] // LANES
    group_rows = rows * n_shells
    high_rows = STATIONS // LANES
    n_high = max(high_rows, n_shells)
    n_devices = n_events * n_shells
    n_chips = n_shells // 2
    two = n_events == 2
    dma = lambda n: pltpu.SemaphoreType.DMA((n,))
    vmem = pl.BlockSpec(memory_space=pltpu.VMEM)
    own, other, correction, weighted = pl.pallas_call(
        functools.partial(whole_kernel, n_events, n_shells),
        out_shape=(
            jax.ShapeDtypeStruct((cells, CELL_BLK), BF16 if two else F32),
            jax.ShapeDtypeStruct((cells if two else GROUP, CELL_BLK), BF16),
            jax.ShapeDtypeStruct((high_rows, LANES), F32),
            jax.ShapeDtypeStruct((rows, LANES), F32),
        ),
        in_specs=[pl.BlockSpec(memory_space=pltpu.SMEM), pl.BlockSpec(memory_space=pl.ANY)]
        + [vmem] * 6,
        out_specs=(vmem,) * 4,
        scratch_shapes=[
            pltpu.VMEM((slots * PICK_BLK, CELL_BLK), BF16),
            pltpu.VMEM((group_rows, slots), BF16),
            pltpu.VMEM((slots, group_rows), BF16),
            pltpu.VMEM((cells, slots), BF16),
            pltpu.VMEM((slots, CELL_BLK), BF16),
            pltpu.VMEM((slots, LANES), F32),
            pltpu.VMEM((slots, LANES), F32),
            pltpu.VMEM((group_rows, LANES), F32),
            pltpu.VMEM((n_chips, rows, LANES), F32),
            pltpu.VMEM((group_rows // 2, LANES), F32),
            pltpu.VMEM((group_rows // 2, LANES), F32),
            pltpu.VMEM((LANES, rows * LANES), BF16),
            pltpu.VMEM((2 * n_high, rows * LANES), BF16),
            pltpu.VMEM((n_high, 2, LANES), F32),
            pltpu.VMEM((n_devices, 2, LANES), F32),
            pltpu.VMEM((n_high, 1, LANES), F32),
            pltpu.VMEM((n_shells, rows, LANES), BF16),
            dma(CHUNKS), dma(1), dma(1),
            dma(n_chips), dma(n_chips), dma(n_devices), dma(n_devices),
            dma(n_shells), dma(n_shells), dma(n_shells), dma(n_shells),
            dma(CHUNKS), dma(CHUNKS),
        ],
        compiler_params=pltpu.CompilerParams(
            collective_id=0, has_side_effects=True, vmem_limit_bytes=60 * 1024 * 1024
        ),
    )(
        blk_count,
        sensitivity.reshape(slots * PICK_BLK, CELL_BLK),
        model.reshape(cells, CELL_BLK),
        pick_block.reshape(1, slots),
        cell_block.reshape(1, slots),
        observed.reshape(rows, LANES),
        pick_weight.reshape(rows, LANES),
        station.reshape(rows, LANES),
    )
    if two:
        gradient, correction, weighted = pl.pallas_call(
            finish_kernel,
            out_shape=(
                jax.ShapeDtypeStruct((cells, CELL_BLK), F32),
                jax.ShapeDtypeStruct((high_rows, LANES), F32),
                jax.ShapeDtypeStruct((rows, LANES), F32),
            ),
            in_specs=[vmem] * 4,
            out_specs=(vmem,) * 3,
            compiler_params=pltpu.CompilerParams(vmem_limit_bytes=60 * 1024 * 1024),
        )(own, other, correction, weighted)
    else:
        gradient = lax.psum(own, "events")
    return (gradient.reshape(-1), correction.reshape(-1), weighted.reshape(-1))


def solution(mesh):
    every = P(("events", "shells"))
    placed = (P("shells"), P(("events", "shells"), None, None)) + (every,) * 6
    return jax.shard_map(
        functools.partial(local, mesh.shape["events"], mesh.shape["shells"]),
        mesh=mesh,
        in_specs=placed,
        out_specs=(P("shells"), P(), every),
        check_vma=False,
    )
```
